32 devices in a mesh: ex: 8 (over z, x), feat: 4 (over y, core).
Axes of the slice: x: 2, y: 2, z: 4, core: 2. Of those that a mesh axis runs over, the one named last changes fastest.
Arguments:
- pooled: bfloat16 [16384, 8192], P('ex', 'feat'), may hold values from -6 to 6
- labels: int32 [16384], P('ex'), may hold values from 0 to 1
- sign_bits: int32 [16384], P('ex'), may hold values from 0 to 1
- margins_old: float32 [16384], P('ex'), may hold values from -8 to 8
- direction: float32 [8192], P(('feat', 'ex')), may hold values from -0.0625 to 0.0625
- sample_rows: int32 [1024], replicated, may hold values from 0 to 16383
Outputs:
- margins: float32 [16384], P('ex')
- gradient: float32 [8192], P(('feat', 'ex'))
- sketch: float32 [1024, 8192], P('ex', 'feat')
The draws below stay inside these ranges and needn't reach their ends.
Inputs may be any that keep to these rules, and one draw needn't show every extreme that they name: `sample_rows`: indices are drawn independently, repeats possible.
All inputs are finite; a program needn't handle non-finite values.
Results may differ from the reference program's by a relative error of at most 0.0033.
Values may be sent and summed in bfloat16 or wider, within the bound.
No kernel may reach another device: no remote copies, remote signals or barrier semaphores. Data moves between devices by JAX's collectives and lax.ppermute only.
A program may use at most 64 MiB of HBM per device.

```python
import math
import jax
import jax.numpy as jnp
from jax import lax

F = 8192
M = 1024
N = 16384


def plant(values, stream_key, smallest, top_value):
    shape = values.shape
    index_at = [jax.random.randint(jax.random.fold_in(stream_key, axis), (), 0, shape[axis]) for axis in range(len(shape))]
    values = values.at[tuple(index_at)].set(smallest)
    longest = shape.index(max(shape))
    index_at[longest] = (index_at[longest] + 1) % shape[longest]
    return values.at[tuple(index_at)].set(top_value)


def strengthened(values, key, source, target, parts, factor):
    owner, partner = [(jnp.arange(values.shape[dim]) // (values.shape[dim] // parts)).reshape([-1 if axis == dim else 1 for axis in range(values.ndim)]) for dim in (source, target)]
    chosen = jax.random.permutation(key, parts)[partner]
    strong = (owner == chosen) | (owner == (partner + parts // 2) % parts)
    return jnp.where(strong, factor * values, values)


def level_of(own_key, extent, shards, smallest, high):
    def one(axis_at, parts):
        draws = jax.random.uniform(jax.random.fold_in(jax.random.fold_in(own_key, 6), axis_at), (parts,), jnp.float32, smallest / len(shards), high / len(shards))
        return jnp.repeat(jnp.exp(draws), extent[axis_at] // parts).reshape((-1,) + (1,) * (len(extent) - axis_at - 1))

    gain = one(*shards[0])
    for cut in shards[1:]:
        gain = gain * one(*cut)
    return gain


def gaussian(key, extent, spread, most, shards=(), kind=jnp.bfloat16):
    drawn = spread * jax.random.normal(key, extent, jnp.float32)
    if shards:
        drawn = drawn * level_of(key, extent, shards, -0.22, 0.18)
    return jnp.clip(drawn, -most, most).astype(kind)


def gaussian_with(key, dims, width, reach, pieces, heavy, held_as=jnp.bfloat16):
    result = width * jax.random.normal(key, dims, jnp.float32)
    if pieces:
        result = result * level_of(key, dims, pieces, -0.22, 0.18)
    return jnp.clip(strengthened(result, jax.random.fold_in(key, 3), *heavy), -reach, reach).astype(held_as)


def setup_inputs(seed: int = 0) -> dict:
    arg_keys = jax.random.split(jax.random.key(seed), 7)
    return {
        "pooled": gaussian_with(arg_keys[0], (N, F), 1.0, 6.0, ((0, 8), (1, 4)), (0, 1, 8, 2.0)),
        "labels": plant(jax.random.randint(arg_keys[1], (N,), 0, 2), jax.random.fold_in(arg_keys[1], 1), 0, 1).astype(jnp.int32),
        "sign_bits": plant(jax.random.randint(arg_keys[2], (N,), 0, 2), jax.random.fold_in(arg_keys[2], 1), 0, 1).astype(jnp.int32),
        "margins_old": gaussian(arg_keys[3], (N,), 2.0, 8.0, ((0, 8),), jnp.float32),
        "direction": gaussian(arg_keys[4], (F,), F ** -0.5, 0.0625, ((0, 32),), jnp.float32),
        "sample_rows": plant(jax.random.randint(arg_keys[5], (M,), 0, N), jax.random.fold_in(arg_keys[5], 1), 0, N - 1).astype(jnp.int32),
    }


col_block = 512

def walsh_rows(column_part):
    row_total = column_part.shape[0]
    half_span = 1
    while half_span < row_total:
        shaped = column_part.reshape(row_total // (2 * half_span), 2, half_span, column_part.shape[1])
        upper_half = shaped[:, 0]
        lower_half = shaped[:, 1]
        column_part = jnp.stack([upper_half + lower_half, upper_half - lower_half], axis=1).reshape(row_total, column_part.shape[1])
        half_span = half_span * 2
    return column_part

def reference(pooled, labels, sign_bits, margins_old, direction, sample_rows):
    step_dir = direction.astype(jnp.bfloat16)
    margins = margins_old + jnp.dot(pooled, step_dir, preferred_element_type=jnp.float32)
    residual = jax.nn.sigmoid(margins) - labels.astype(jnp.float32)
    weight = jnp.sqrt(jax.nn.sigmoid(margins) * jax.nn.sigmoid(-margins))
    gradient = jnp.dot(residual.astype(jnp.bfloat16), pooled, preferred_element_type=jnp.float32) / math.sqrt(N)
    scale_rows = (2 * sign_bits - 1).astype(jnp.float32) * weight
    weighted = (pooled * scale_rows[:, None]).astype(jnp.bfloat16)
    stacked = weighted.reshape(N, F // col_block, col_block).transpose(1, 0, 2)

    def one_block(column_part):
        return walsh_rows(column_part.astype(jnp.float32))[sample_rows]
    picked = lax.map(one_block, stacked)
    sketch = picked.transpose(1, 0, 2).reshape(M, F) / math.sqrt(M)
    return (margins, gradient, sketch)
```

```python
import functools
import math

import jax
import jax.numpy as jnp
from jax import lax
from jax.experimental import pallas as pl
from jax.experimental.pallas import tpu as pltpu
from jax.sharding import PartitionSpec as P

LANES = 128
VMEM_LIMIT = 48 * 1024 * 1024
PARAMS = pltpu.CompilerParams(vmem_limit_bytes=VMEM_LIMIT)


def tile_of(extent, most):
    size = most
    while extent % size:
        size //= 2
    return size


def swap_with(value, axis, distance):
    count = lax.axis_size(axis)
    return lax.ppermute(value, axis, [(i, i ^ distance) for i in range(count)])


def send_order(bits):
    rounds = []
    for bit in range(bits):
        blocks = [r for r in range(1 << bits) if r & ((2 << bit) - 1) == 1 << bit]
        blocks.sort(key=lambda r: [-(r >> b & 1) for b in range(bit + 1, bits)])
        rounds.append(blocks)
    return rounds


def margins_kernel(dir_ref, pooled_ref, out_ref):
    row = lax.dot_general(
        dir_ref[...], pooled_ref[...], (((1,), (1,)), ((), ())), preferred_element_type=jnp.float32
    )
    for part in range(pooled_ref.shape[0] // LANES):
        out_ref[0, part : part + 1, :] = row[0:1, part * LANES : (part + 1) * LANES]


def partial_margins(pooled, step_dir):
    rows, cols = pooled.shape
    tile = tile_of(rows, 256)
    out = pl.pallas_call(
        margins_kernel,
        grid=(rows // tile,),
        in_specs=[
            pl.BlockSpec((8, cols), lambda i: (0, 0)),
            pl.BlockSpec((tile, cols), lambda i: (i, 0)),
        ],
        out_specs=pl.BlockSpec((1, tile // LANES, LANES), lambda i: (i, 0, 0)),
        out_shape=jax.ShapeDtypeStruct((rows // tile, tile // LANES, LANES), jnp.float32),
        compiler_params=PARAMS,
        cost_estimate=pl.CostEstimate(flops=2 * rows * cols, bytes_accessed=2 * rows * cols, transcendentals=0),
        name="margins",
    )(jnp.broadcast_to(step_dir[None, :], (8, cols)), pooled)
    return out.reshape(rows // LANES, LANES)


def fill_signs(signs_ref, sampled, ex_index, row_count):
    high_bits = row_count.bit_length() - 1
    lane = lax.broadcasted_iota(jnp.int32, sampled.shape, 1)
    folded = (sampled & lane) ^ (lax.shift_right_logical(sampled, high_bits) & ex_index)
    for shift_by in (16, 8, 4, 2, 1):
        folded = folded ^ lax.shift_right_logical(folded, shift_by)
    tiles = [(1 - 2 * (folded & 1)).astype(jnp.float32)]
    for bit in range(LANES.bit_length() - 1, high_bits):
        flip = (1 - 2 * (lax.shift_right_logical(sampled, bit) & 1)).astype(jnp.float32)
        tiles = tiles + [tile * flip for tile in tiles]
    for at, tile in enumerate(tiles):
        signs_ref[:, at * LANES : (at + 1) * LANES] = tile.astype(jnp.bfloat16)


def fill_scale(scale_col_ref, scale):
    groups = scale.shape[0]
    for at in range(groups):
        square = jnp.broadcast_to(scale[at : at + 1, :], (LANES, LANES))
        scale_col_ref[at * LANES : (at + 1) * LANES, :] = square.T


def weigh(pooled_ref, scale_col_ref):
    pieces = []
    for at in range(pooled_ref.shape[1] // LANES):
        part = pooled_ref[:, at * LANES : (at + 1) * LANES].astype(jnp.float32)
        pieces.append((part * scale_col_ref[...]).astype(jnp.bfloat16))
    return pieces[0] if len(pieces) == 1 else jnp.concatenate(pieces, axis=1)


def first_kernel(
    block_rows, ex_ref, mine_ref, theirs_ref, old_ref, labels_ref, bits_ref, sampled_ref, pooled_ref, *rest
):
    *outs, margins_ref, scale_ref, residual_ref, signs_ref, scale_col_ref = rest

    @pl.when(pl.program_id(0) == 0)
    def _():
        margins = old_ref[...] + (mine_ref[...] + theirs_ref[...])
        up, down = jax.nn.sigmoid(margins), jax.nn.sigmoid(-margins)
        scale = (2 * bits_ref[...] - 1).astype(jnp.float32) * jnp.sqrt(up * down)
        margins_ref[...] = margins
        scale_ref[...] = scale
        residual_ref[...] = up - labels_ref[...].astype(jnp.float32)
        fill_scale(scale_col_ref, scale)
        fill_signs(signs_ref, sampled_ref[...], ex_ref[0], pooled_ref.shape[0])

    weighted = weigh(pooled_ref, scale_col_ref)
    terms = jnp.dot(signs_ref[...], weighted, preferred_element_type=jnp.float32)
    for at, out in enumerate(outs):
        out[...] = terms[at * block_rows : (at + 1) * block_rows].astype(out.dtype)


def rest_kernel(block_rows, ex_ref, scale_ref, sampled_ref, pooled_ref, *rest):
    *outs, signs_ref, scale_col_ref = rest

    @pl.when(pl.program_id(0) == 0)
    def _():
        fill_scale(scale_col_ref, scale_ref[...])
        fill_signs(signs_ref, sampled_ref[...], ex_ref[0], pooled_ref.shape[0])

    weighted = weigh(pooled_ref, scale_col_ref)
    terms = jnp.dot(signs_ref[...], weighted, preferred_element_type=jnp.float32)
    for at, out in enumerate(outs):
        out[...] = terms[at * block_rows : (at + 1) * block_rows].astype(out.dtype)


def whole_spec(shape):
    return pl.BlockSpec(shape, lambda i: (0,) * len(shape))


def sketch_terms(kernel, name, ex_index, small, sampled, pooled, block_rows, kinds, extra=()):
    rows, cols = pooled.shape
    tile = tile_of(cols, 256)
    smem = pl.BlockSpec(memory_space=pltpu.SMEM)
    out_shape = [jax.ShapeDtypeStruct((block_rows, cols), kind) for kind in kinds]
    out_specs = [pl.BlockSpec((block_rows, tile), lambda i: (0, i)) for _ in kinds]
    out_shape += [jax.ShapeDtypeStruct(shape, jnp.float32) for shape in extra]
    out_specs += [whole_spec(shape) for shape in extra]
    return pl.pallas_call(
        functools.partial(kernel, block_rows),
        grid=(cols // tile,),
        in_specs=[smem]
        + [whole_spec(x.shape) for x in small]
        + [whole_spec(sampled.shape), pl.BlockSpec((rows, tile), lambda i: (0, i))],
        out_specs=out_specs,
        out_shape=out_shape,
        scratch_shapes=[
            pltpu.VMEM((sampled.shape[0], rows), jnp.bfloat16),
            pltpu.VMEM((rows, LANES), jnp.float32),
        ],
        compiler_params=PARAMS,
        cost_estimate=pl.CostEstimate(
            flops=2 * sampled.shape[0] * rows * cols, bytes_accessed=2 * rows * cols, transcendentals=0
        ),
        name=name,
    )(ex_index, *small, sampled, pooled)


def gradient_kernel(residual_ref, pooled_ref, out_ref):
    row = jnp.concatenate([residual_ref[at : at + 1, :] for at in range(residual_ref.shape[0])], axis=1)
    left = jnp.broadcast_to(row, (8, row.shape[1])).astype(jnp.bfloat16)
    out_ref[...] = jnp.dot(left, pooled_ref[...], preferred_element_type=jnp.float32)[0:1, :]


def gradient_terms(residual, pooled):
    rows, cols = pooled.shape
    tile = tile_of(cols, 256)
    return pl.pallas_call(
        gradient_kernel,
        grid=(cols // tile,),
        in_specs=[whole_spec(residual.shape), pl.BlockSpec((rows, tile), lambda i: (0, i))],
        out_specs=pl.BlockSpec((1, tile), lambda i: (0, i)),
        out_shape=jax.ShapeDtypeStruct((1, cols), jnp.float32),
        compiler_params=PARAMS,
        cost_estimate=pl.CostEstimate(flops=2 * rows * cols, bytes_accessed=2 * rows * cols, transcendentals=0),
        name="gradient",
    )(residual, pooled)


def flipped_by(value, index, bits):
    tail = value.shape[1:]
    cube = value.reshape((2,) * bits + tail)
    for bit in range(bits):
        axis = bits - 1 - bit
        cube = jnp.where((index >> bit) & 1 == 1, jnp.flip(cube, axis), cube)
    return cube.reshape((1 << bits,) + tail)


def on_device(pooled, labels, sign_bits, margins_old, direction, sample_rows):
    rows, cols = pooled.shape
    ex_count, feat_count = lax.axis_size("ex"), lax.axis_size("feat")
    bits = ex_count.bit_length() - 1
    ex_index = lax.axis_index("ex").astype(jnp.int32)
    total_rows = rows * ex_count
    sketch_count = sample_rows.shape[0]
    block_rows = sketch_count // ex_count
    dense = (rows // LANES, LANES)

    step_dir = direction.astype(jnp.bfloat16)
    for bit in range(bits):
        other = swap_with(step_dir, "ex", 1 << bit)
        low = (ex_index >> bit) & 1 == 0
        step_dir = jnp.concatenate([jnp.where(low, step_dir, other), jnp.where(low, other, step_dir)])

    terms = partial_margins(pooled, step_dir)
    distance = 1
    while distance < feat_count:
        mine, theirs = terms, swap_with(terms, "feat", distance)
        terms = mine + theirs
        distance *= 2

    order = send_order(bits)
    early = order[0][:2]
    late = [r for r in range(ex_count) if r not in early]
    leaving_at_once = set(order[0])
    by_owner = flipped_by(sample_rows.reshape(ex_count, block_rows), ex_index, bits)

    def sampled_of(blocks):
        picked = jnp.concatenate([by_owner[r] for r in blocks])
        return jnp.broadcast_to(picked[:, None], (picked.shape[0], LANES))

    def kinds_of(blocks):
        return [jnp.bfloat16 if r in leaving_at_once else jnp.float32 for r in blocks]

    ex_scalar = ex_index.reshape(1)
    *first, margins, scale, residual = sketch_terms(
        first_kernel,
        "first_terms",
        ex_scalar,
        [mine, theirs, margins_old.reshape(dense), labels.reshape(dense), sign_bits.reshape(dense)],
        sampled_of(early),
        pooled,
        block_rows,
        kinds_of(early),
        extra=[dense] * 3,
    )
    rest = sketch_terms(
        rest_kernel, "rest_terms", ex_scalar, [scale], sampled_of(late), pooled, block_rows, kinds_of(late)
    )
    held = dict(zip(early, first)) | dict(zip(late, rest))

    for bit, blocks in enumerate(order):
        for r in blocks:
            arrived = swap_with(held.pop(r).astype(jnp.bfloat16), "ex", 1 << bit)
            kept = r ^ (1 << bit)
            held[kept] = held[kept] + arrived.astype(jnp.float32)
    sketch = held[0] * (1 / math.sqrt(sketch_count))

    part = gradient_terms(residual, pooled)[0]
    for bit in reversed(range(bits)):
        low = (ex_index >> bit) & 1 == 0
        lower, upper = jnp.split(part, 2)
        arrived = swap_with(jnp.where(low, upper, lower), "ex", 1 << bit)
        part = jnp.where(low, lower, upper) + arrived
    gradient = part / math.sqrt(total_rows)
    return margins.reshape(rows), gradient, sketch


def solution(mesh):
    return jax.shard_map(
        on_device,
        mesh=mesh,
        in_specs=(P("ex", "feat"), P("ex"), P("ex"), P("ex"), P(("feat", "ex")), P()),
        out_specs=(P("ex"), P(("feat", "ex")), P("ex", "feat")),
        check_vma=False,
    )
```

```python
import functools
import math

import jax
import jax.numpy as jnp
from jax import lax
from jax.experimental import pallas as pl
from jax.experimental.pallas import tpu as pltpu
from jax.sharding import PartitionSpec as P

LANES = 128
VMEM_LIMIT = 40 * 1024 * 1024
PARAMS = pltpu.CompilerParams(vmem_limit_bytes=VMEM_LIMIT)


def tile_of(extent, most):
    size = most
    while extent % size:
        size //= 2
    return size


def swap_with(value, axis, distance):
    count = lax.axis_size(axis)
    return lax.ppermute(value, axis, [(i, i ^ distance) for i in range(count)])


def call_in_vmem(kernel, name, out_shape, scratch, flops, *operands, scalars=()):
    vmem, smem = pl.BlockSpec(memory_space=pltpu.VMEM), pl.BlockSpec(memory_space=pltpu.SMEM)
    return pl.pallas_call(
        kernel,
        in_specs=[smem] * len(scalars) + [vmem] * len(operands),
        out_specs=[vmem] * len(out_shape),
        out_shape=[jax.ShapeDtypeStruct(*entry) for entry in out_shape],
        scratch_shapes=scratch,
        compiler_params=PARAMS,
        cost_estimate=pl.CostEstimate(flops=0, bytes_accessed=0, transcendentals=0),
        name=name,
    )(*scalars, *(x if x.size < 1 << 18 else pltpu.with_memory_space_constraint(x, pltpu.VMEM) for x in operands))


def margins_kernel(dir_ref, pooled_ref, out_ref):
    rows = pooled_ref.shape[0]
    tile = tile_of(rows, 512)
    for at in range(0, rows, tile):
        row = lax.dot_general(
            dir_ref[...],
            pooled_ref[at : at + tile, :],
            (((1,), (1,)), ((), ())),
            preferred_element_type=jnp.float32,
        )
        for part in range(0, tile, LANES):
            group = (at + part) // LANES
            out_ref[group : group + 1, :] = row[0:1, part : part + LANES]


def fill_signs(signs_ref, sampled, ex_index):
    high_bits = signs_ref.shape[1].bit_length() - 1
    lane = lax.broadcasted_iota(jnp.int32, sampled.shape, 1)
    folded = (sampled & lane) ^ (lax.shift_right_logical(sampled, high_bits) & ex_index)
    for shift_by in (16, 8, 4, 2, 1):
        folded = folded ^ lax.shift_right_logical(folded, shift_by)
    tiles = [(1 - 2 * (folded & 1)).astype(jnp.float32)]
    for bit in range(LANES.bit_length() - 1, high_bits):
        flip = (1 - 2 * (lax.shift_right_logical(sampled, bit) & 1)).astype(jnp.float32)
        tiles = tiles + [tile * flip for tile in tiles]
    for at, tile in enumerate(tiles):
        signs_ref[:, at * LANES : (at + 1) * LANES] = tile.astype(jnp.bfloat16)


def fill_scale(scale_col_ref, scale):
    for at in range(scale.shape[0]):
        square = jnp.broadcast_to(scale[at : at + 1, :], (LANES, LANES))
        scale_col_ref[at * LANES : (at + 1) * LANES, :] = square.T


def weigh(pooled, scale_col):
    pieces = []
    for at in range(0, pooled.shape[1], LANES):
        part = pooled[:, at : at + LANES].astype(jnp.float32)
        pieces.append((part * scale_col).astype(jnp.bfloat16))
    return pieces[0] if len(pieces) == 1 else jnp.concatenate(pieces, axis=1)


def write_terms(cols, block_rows, pooled_ref, signs_ref, scale_col_ref, outs):
    tile = tile_of(cols, 256)
    for at in range(0, cols, tile):
        weighted = weigh(pooled_ref[:, at : at + tile], scale_col_ref[...])
        terms = jnp.dot(signs_ref[...], weighted, preferred_element_type=jnp.float32)
        for k, out in enumerate(outs):
            out[:, at : at + tile] = terms[k * block_rows : (k + 1) * block_rows].astype(out.dtype)


def first_kernel(
    cols, block_rows, ex_ref, mine_ref, theirs_ref, old_ref, labels_ref, bits_ref, sampled_ref, pooled_ref, *rest
):
    *outs, margins_ref, scale_ref, residual_ref, signs_ref, scale_col_ref = rest
    margins = old_ref[...] + (mine_ref[...] + theirs_ref[...])
    up, down = jax.nn.sigmoid(margins), jax.nn.sigmoid(-margins)
    scale = (2 * bits_ref[...] - 1).astype(jnp.float32) * jnp.sqrt(up * down)
    margins_ref[...] = margins
    scale_ref[...] = scale
    residual_ref[...] = up - labels_ref[...].astype(jnp.float32)
    fill_scale(scale_col_ref, scale)
    fill_signs(signs_ref, sampled_ref[...], ex_ref[0])
    write_terms(cols, block_rows, pooled_ref, signs_ref, scale_col_ref, outs)


def more_kernel(cols, block_rows, ex_ref, scale_ref, sampled_ref, pooled_ref, *rest):
    *outs, signs_ref, scale_col_ref = rest
    fill_scale(scale_col_ref, scale_ref[...])
    fill_signs(signs_ref, sampled_ref[...], ex_ref[0])
    write_terms(cols, block_rows, pooled_ref, signs_ref, scale_col_ref, outs)


def terms_of(kernel, name, cols, block_rows, ex_scalar, small, sampled, pooled, kinds, extra=()):
    rows = pooled.shape[0]
    return call_in_vmem(
        functools.partial(kernel, cols, block_rows),
        name,
        [((block_rows, cols), kind) for kind in kinds] + [(shape, jnp.float32) for shape in extra],
        [pltpu.VMEM((sampled.shape[0], rows), jnp.bfloat16), pltpu.VMEM((rows, LANES), jnp.float32)],
        2 * sampled.shape[0] * rows * cols,
        *small,
        sampled,
        pooled,
        scalars=(ex_scalar,),
    )


def pair_kernel(first_col, ex_ref, scale_ref, scale2_ref, sampled_ref, pooled_ref, theirs_ref, *rest):
    *outs, signs_ref, scale_col_ref = rest
    half = theirs_ref.shape[1]
    high_bits = signs_ref.shape[1].bit_length() - 1
    fill_signs(signs_ref, sampled_ref[...], ex_ref[0])
    flip = (1 - 2 * (lax.shift_right_logical(sampled_ref[...], high_bits) & 1)).astype(jnp.float32)
    start = pl.multiple_of(first_col + (ex_ref[0] & 1) * half, LANES)
    fill_scale(scale_col_ref, scale_ref[...])
    own = jnp.dot(
        signs_ref[...],
        weigh(pooled_ref[:, pl.ds(start, half)], scale_col_ref[...]),
        preferred_element_type=jnp.float32,
    )
    fill_scale(scale_col_ref, scale2_ref[...])
    other = jnp.dot(
        signs_ref[...], weigh(theirs_ref[...], scale_col_ref[...]), preferred_element_type=jnp.float32
    )
    for at in range(0, half, LANES):
        terms = own[:, at : at + LANES] + flip * other[:, at : at + LANES]
        row = 0
        for out in outs:
            out[:, at : at + LANES] = terms[row : row + out.shape[0]].astype(out.dtype)
            row += out.shape[0]


def gradient_kernel(residual_ref, pooled_ref, out_ref):
    row = jnp.concatenate([residual_ref[at : at + 1, :] for at in range(residual_ref.shape[0])], axis=1)
    left = jnp.broadcast_to(row, (8, row.shape[1])).astype(jnp.bfloat16)
    tile = tile_of(pooled_ref.shape[1], 512)
    for at in range(0, pooled_ref.shape[1], tile):
        terms = jnp.dot(left, pooled_ref[:, at : at + tile], preferred_element_type=jnp.float32)
        out_ref[:, at : at + tile] = terms[0:1, :]


def flipped_by(value, index, bits):
    tail = value.shape[1:]
    cube = value.reshape((2,) * bits + tail)
    for bit in range(bits):
        axis = bits - 1 - bit
        cube = jnp.where((index >> bit) & 1 == 1, jnp.flip(cube, axis), cube)
    return cube.reshape((1 << bits,) + tail)


def after(value, *others):
    return lax.optimization_barrier((value, *others))[0]


def wide(value):
    return value.astype(jnp.float32)


def on_device(pooled, labels, sign_bits, margins_old, direction, sample_rows):
    rows, cols = pooled.shape
    ex_count, feat_count = lax.axis_size("ex"), lax.axis_size("feat")
    bits = ex_count.bit_length() - 1
    ex_index = lax.axis_index("ex").astype(jnp.int32)
    total_rows = rows * ex_count
    sketch_count = sample_rows.shape[0]
    block_rows = sketch_count // ex_count
    dense = (rows // LANES, LANES)
    half = cols // 8 if cols % (8 * LANES) == 0 and bits > 1 else 0
    plain = cols - 2 * half
    odd = ex_index & 1 == 1

    step_dir = direction
    raw = None
    for bit in range(bits):
        other = swap_with(step_dir.astype(jnp.bfloat16), "ex", 1 << bit)
        low = (ex_index >> bit) & 1 == 0
        own = step_dir.astype(jnp.bfloat16)
        step_dir = jnp.concatenate([jnp.where(low, own, other), jnp.where(low, other, own)])
        if half and raw is None:
            leaving = jnp.where(odd, pooled[:, plain : plain + half], pooled[:, plain + half :])
            raw = swap_with(after(leaving, other), "ex", 1)

    (terms,) = call_in_vmem(
        margins_kernel,
        "margins",
        [(dense, jnp.float32)],
        [],
        2 * rows * cols,
        jnp.broadcast_to(step_dir[None, :], (8, cols)),
        pooled,
    )
    mine, theirs = terms, jnp.zeros_like(terms)
    distance = 1
    while distance < feat_count:
        mine = terms
        theirs = swap_with(mine, "feat", distance)
        terms = mine + theirs
        distance *= 2

    by_owner = flipped_by(sample_rows.reshape(ex_count, block_rows), ex_index, bits)
    order = [[r for r in range(ex_count - 1, 0, -1) if r & ((2 << bit) - 1) == 1 << bit] for bit in range(bits)]
    first = order[0][:1]
    second = order[0][1:2] + [order[0][0] ^ 1]
    third = [r for r in range(ex_count) if r not in first + second]

    def sampled_of(blocks):
        picked = jnp.concatenate([by_owner[r] for r in blocks])
        return jnp.broadcast_to(picked[:, None], (picked.shape[0], LANES))

    def kinds_of(blocks):
        return [jnp.bfloat16 if r & 1 else jnp.float32 for r in blocks]

    ex_scalar = ex_index.reshape(1)
    *made, margins, scale, residual = terms_of(
        first_kernel,
        "first_terms",
        plain,
        block_rows,
        ex_scalar,
        [mine, theirs, margins_old.reshape(dense), labels.reshape(dense), sign_bits.reshape(dense)],
        sampled_of(first),
        pooled,
        kinds_of(first),
        extra=[dense] * 3,
    )
    held = dict(zip(first, made))
    if half:
        scale_theirs = swap_with(scale, "ex", 1)

    def more(blocks, name, scale):
        if blocks:
            made = terms_of(
                more_kernel, name, plain, block_rows, ex_scalar, [scale], sampled_of(blocks), pooled, kinds_of(blocks)
            )
            held.update(zip(blocks, made))

    more(second, "second_terms", after(scale, raw) if half else scale)

    if half:
        groups, left = [], sorted(range(ex_count), key=lambda r: [r >> b & 1 for b in (*range(1, bits), 0)])
        for bit in range(1, bits):
            groups.append([r for r in left if r >> bit & 1])
            left = [r for r in left if not r >> bit & 1]
        groups += [[1], [0]]
        pair = call_in_vmem(
            functools.partial(pair_kernel, plain),
            "pair_terms",
            [
                ((len(group) * block_rows, half), jnp.bfloat16 if at == 0 else jnp.float32)
                for at, group in enumerate(groups)
            ],
            [pltpu.VMEM((sketch_count, rows), jnp.bfloat16), pltpu.VMEM((rows, LANES), jnp.float32)],
            4 * sketch_count * rows * half,
            after(scale, *held.values()),
            scale_theirs,
            sampled_of([r for group in groups for r in group]),
            pooled,
            raw,
            scalars=(ex_scalar,),
        )
        pair = [wide(x) for x in pair]
        for at in range(bits - 1):
            arrived = wide(swap_with(pair[at].astype(jnp.bfloat16), "ex", 2 << at))
            row = 0
            for later in range(bits, at, -1):
                size = pair[later].shape[0]
                pair[later] = pair[later] + arrived[row : row + size]
                row += size
        moved = wide(swap_with(pair[-2].astype(jnp.bfloat16), "ex", 1))

    def exchange(r):
        bit = (r & -r).bit_length() - 1
        arrived = wide(swap_with(held.pop(r).astype(jnp.bfloat16), "ex", 1 << bit))
        held[r ^ (1 << bit)] = held[r ^ (1 << bit)] + arrived

    exchange(order[0][0])
    more(third, "third_terms", after(scale, held[order[0][0] ^ 1]))
    held_late = [held[0]]
    for bit, blocks in enumerate(order):
        for r in blocks:
            if r in held:
                exchange(r)
            if bit == bits - 2 and r == blocks[0]:
                held_late = [held[r ^ (1 << bit)]]
    sketch = held[0]
    if half:
        sketch = jnp.concatenate(
            [sketch, jnp.where(odd, moved, pair[-1]), jnp.where(odd, pair[-1], moved)], axis=1
        )
    sketch = sketch * (1 / math.sqrt(sketch_count))

    (part,) = call_in_vmem(
        gradient_kernel,
        "gradient",
        [((1, cols), jnp.float32)],
        [],
        2 * rows * cols,
        after(residual, *held_late),
        pooled,
    )
    part = part[0]
    for bit in reversed(range(bits)):
        low = (ex_index >> bit) & 1 == 0
        lower, upper = jnp.split(part, 2)
        arrived = swap_with(jnp.where(low, upper, lower), "ex", 1 << bit)
        part = jnp.where(low, lower, upper) + arrived
    gradient = part / math.sqrt(total_rows)
    return margins.reshape(rows), gradient, sketch


def solution(mesh):
    return jax.shard_map(
        on_device,
        mesh=mesh,
        in_specs=(P("ex", "feat"), P("ex"), P("ex"), P("ex"), P(("feat", "ex")), P()),
        out_specs=(P("ex"), P(("feat", "ex")), P("ex", "feat")),
        check_vma=False,
    )
```

```python
import functools
import math

import jax
import jax.numpy as jnp
from jax import lax
from jax.experimental import pallas as pl
from jax.experimental.pallas import tpu as pltpu
from jax.sharding import PartitionSpec as P

LANES = 128
PARAMS = pltpu.CompilerParams(vmem_limit_bytes=40 * 1024 * 1024)
NO_COST = pl.CostEstimate(flops=0, bytes_accessed=0, transcendentals=0)
ANY = pl.BlockSpec(memory_space=pl.ANY)
VMEM = pl.BlockSpec(memory_space=pltpu.VMEM)
SMEM = pl.BlockSpec(memory_space=pltpu.SMEM)


def tile_of(extent, most):
    size = most
    while extent % size:
        size //= 2
    return size


def swap_with(value, axis, distance):
    count = lax.axis_size(axis)
    return lax.ppermute(value, axis, [(i, i ^ distance) for i in range(count)])


def wide(value):
    return value.astype(jnp.float32)


def narrow(value):
    return value.astype(jnp.bfloat16)


def call(kernel, name, out_shape, scratch, *operands, scalars=(), whole=(), large=(), deps=()):
    large = [pltpu.with_memory_space_constraint(x, pltpu.VMEM) for x in large]
    used = len(scalars) + len(operands) + len(large) + len(whole)
    return pl.pallas_call(
        lambda *refs: kernel(*refs[:used], *refs[used + len(deps) :]),
        in_specs=[SMEM] * len(scalars) + [VMEM] * (len(operands) + len(large)) + [ANY] * (len(whole) + len(deps)),
        out_specs=[VMEM] * len(out_shape),
        out_shape=[jax.ShapeDtypeStruct(*entry) for entry in out_shape],
        scratch_shapes=scratch,
        compiler_params=PARAMS,
        cost_estimate=NO_COST,
        name=name,
    )(*scalars, *operands, *large, *whole, *deps)


def margins_kernel(pieces, ex_ref, dir_ref, pooled_ref, out_ref, ordered_ref):
    rows, cols = pooled_ref.shape
    tile, width = tile_of(rows, 512), cols // pieces
    lanes = dir_ref.shape[1]
    for at in range(dir_ref.shape[0]):
        piece = jnp.broadcast_to(dir_ref[at : at + 1, :], (8, lanes))
        r, part = divmod(at * lanes, width)
        place = pl.ds(pl.multiple_of((ex_ref[0] ^ r) * width + part, lanes), lanes) if pieces > 1 else slice(None)
        ordered_ref[:, place] = piece
    left = ordered_ref[...].astype(jnp.bfloat16)
    for at in range(0, rows, tile):
        row = lax.dot_general(
            left, pooled_ref[at : at + tile, :], (((1,), (1,)), ((), ())), preferred_element_type=jnp.float32
        )
        for part in range(0, tile, LANES):
            group = (at + part) // LANES
            out_ref[group : group + 1, :] = row[0:1, part : part + LANES]


def sampled_rows(sampled_ref, ex_index, blocks):
    columns = []
    for r in blocks:
        row = sampled_ref[pl.ds(ex_index ^ r, 1), :]
        columns.append(jnp.broadcast_to(row, (LANES, row.shape[1])).T)
    return columns[0] if len(columns) == 1 else jnp.concatenate(columns)


def fill_signs(signs_ref, sampled, ex_index):
    high_bits = signs_ref.shape[1].bit_length() - 1
    lane = lax.broadcasted_iota(jnp.int32, sampled.shape, 1)
    folded = (sampled & lane) ^ (lax.shift_right_logical(sampled, high_bits) & ex_index)
    for shift_by in (16, 8, 4, 2, 1):
        folded = folded ^ lax.shift_right_logical(folded, shift_by)
    tiles = [(1 - 2 * (folded & 1)).astype(jnp.float32)]
    for bit in range(LANES.bit_length() - 1, high_bits):
        flip = (1 - 2 * (lax.shift_right_logical(sampled, bit) & 1)).astype(jnp.float32)
        tiles = tiles + [tile * flip for tile in tiles]
    for at, tile in enumerate(tiles):
        signs_ref[:, at * LANES : (at + 1) * LANES] = tile.astype(jnp.bfloat16)


def fill_scale(scale_col_ref, scale):
    for at in range(scale.shape[0]):
        square = jnp.broadcast_to(scale[at : at + 1, :], (LANES, LANES))
        scale_col_ref[at * LANES : (at + 1) * LANES, :] = square.T


def weigh(pooled, scale_col):
    pieces = []
    for at in range(0, pooled.shape[1], LANES):
        part = pooled[:, at : at + LANES].astype(jnp.float32)
        pieces.append((part * scale_col).astype(jnp.bfloat16))
    return pieces[0] if len(pieces) == 1 else jnp.concatenate(pieces, axis=1)


def weights_kernel(mine_ref, theirs_ref, old_ref, labels_ref, bits_ref, margins_ref, scale_ref, residual_ref):
    margins = old_ref[...] + (mine_ref[...] + theirs_ref[...])
    up, down = jax.nn.sigmoid(margins), jax.nn.sigmoid(-margins)
    margins_ref[...] = margins
    scale_ref[...] = (2 * bits_ref[...] - 1).astype(jnp.float32) * jnp.sqrt(up * down)
    residual_ref[...] = up - labels_ref[...].astype(jnp.float32)


def terms_kernel(places, blocks, ex_ref, scale_ref, sampled_ref, pooled_ref, *rest):
    *outs, signs_ref, scale_col_ref = rest
    cols = pooled_ref.shape[1]
    tile = tile_of(cols, 256)
    fill_scale(scale_col_ref, scale_ref[...])
    fill_signs(signs_ref, sampled_rows(sampled_ref, ex_ref[0], blocks), ex_ref[0])
    for at in range(0, cols, tile):
        weighted = weigh(pooled_ref[:, at : at + tile], scale_col_ref[...])
        terms = jnp.dot(signs_ref[...], weighted, preferred_element_type=jnp.float32)
        for (row, col), out in zip(places, outs):
            if col <= at < col + out.shape[1]:
                out[:, at - col : at - col + tile] = terms[row : row + out.shape[0]].astype(out.dtype)


def terms_of(name, blocks, ex_scalar, scale, sampled, pooled, places, outs, deps=()):
    rows, block_rows = pooled.shape[0], sampled.shape[1]
    return call(
        functools.partial(terms_kernel, places, blocks),
        name,
        outs,
        [
            pltpu.VMEM((len(blocks) * block_rows, rows), jnp.bfloat16),
            pltpu.VMEM((rows, LANES), jnp.float32),
        ],
        scale,
        sampled,
        scalars=(ex_scalar,),
        large=(pooled,),
        deps=deps,
    )


def gradient_kernel(residual_ref, pooled_ref, out_ref):
    row = jnp.concatenate([residual_ref[at : at + 1, :] for at in range(residual_ref.shape[0])], axis=1)
    left = jnp.broadcast_to(row, (8, row.shape[1])).astype(jnp.bfloat16)
    tile = tile_of(pooled_ref.shape[1], 512)
    for at in range(0, pooled_ref.shape[1], tile):
        terms = jnp.dot(left, pooled_ref[:, at : at + tile], preferred_element_type=jnp.float32)
        out_ref[:, at : at + tile] = terms[0:1, :]


def finish_kernel(counts, scales, *refs):
    *ins, sketch_ref, gradient_ref = refs
    col = 0
    ins = list(ins)
    for count, offsets in counts:
        group, ins = ins[:count], ins[count:]
        width = group[0].shape[1]
        total = group[0][...]
        for ref, offset in zip(group[1:], offsets):
            total = total + wide(ref[:, offset : offset + width])
        sketch_ref[:, col : col + width] = total * scales[0]
        col += width
    gradient_ref[...] = (ins[-2][...] + ins[-1][...]) * scales[1]


def on_device(pooled, labels, sign_bits, margins_old, direction, sample_rows):
    rows, cols = pooled.shape
    ex_count, feat_count = lax.axis_size("ex"), lax.axis_size("feat")
    bits = ex_count.bit_length() - 1
    ex_index = lax.axis_index("ex").astype(jnp.int32)
    ex_scalar = ex_index.reshape(1)
    sketch_count = sample_rows.shape[0]
    block_rows = sketch_count // ex_count
    dense = (rows // LANES, LANES)
    sampled = sample_rows.reshape(ex_count, block_rows)
    pieces = ex_count if direction.shape[0] % LANES == 0 else 1
    step_dir = direction.reshape(-1, LANES) if pieces > 1 else direction
    for bit in range(bits):
        other = swap_with(step_dir, "ex", 1 << bit)
        if pieces > 1:
            step_dir = jnp.concatenate([step_dir, other])
        else:
            low = (ex_index >> bit) & 1 == 0
            step_dir = jnp.concatenate([jnp.where(low, step_dir, other), jnp.where(low, other, step_dir)])

    (terms,) = call(
        functools.partial(margins_kernel, pieces),
        "margins",
        [(dense, jnp.float32)],
        [pltpu.VMEM((8, cols), jnp.float32)],
        step_dir if pieces > 1 else step_dir.reshape(1, cols),
        scalars=(ex_scalar,),
        large=(pooled,),
    )
    mine, theirs = terms, jnp.zeros_like(terms)
    distance = 1
    while distance < feat_count:
        mine, theirs = terms, swap_with(terms, "feat", distance)
        terms = mine + theirs
        distance *= 2

    margins, scale, residual = call(
        weights_kernel,
        "weights",
        [(dense, jnp.float32)] * 3,
        [],
        mine,
        theirs,
        margins_old.reshape(dense),
        labels.reshape(dense),
        sign_bits.reshape(dense),
    )
    order = [[r for r in range(ex_count - 1, 0, -1) if r & ((2 << bit) - 1) == 1 << bit] for bit in range(bits)]
    first = order[0][:2]
    cut = cols // 2 // (2 * LANES) * (2 * LANES) or cols
    spans = [(0, cut), (cut, cols)] if cut < cols else [(0, cols)]
    made = terms_of(
        "first_terms",
        first,
        ex_scalar,
        scale,
        sampled,
        pooled,
        [(0, begin) for begin, _ in spans],
        [((len(first) * block_rows, end - begin), jnp.bfloat16) for begin, end in spans],
    )
    last = made
    arrived_first = [swap_with(x, "ex", 1) for x in made]

    (part,) = call(
        gradient_kernel,
        "gradient",
        [((1, cols), jnp.float32)],
        [],
        residual,
        large=(pooled,),
        deps=last[:1],
    )
    last = [part]
    part = part.reshape(-1)

    own, arrivals = {}, {r: [] for r in range(ex_count)}

    def more(blocks, name, deps):
        cuts = [(k, r, span) for k, r in enumerate(blocks) for span in (spans if r in parted else [(0, cols)])]
        made = terms_of(
            name,
            blocks,
            ex_scalar,
            scale,
            sampled,
            pooled,
            [(k * block_rows, begin) for k, _, (begin, _) in cuts],
            [((block_rows, end - begin), jnp.bfloat16 if r & 1 else jnp.float32) for _, r, (begin, end) in cuts],
            deps,
        )
        for (_, r, (begin, _)), value in zip(cuts, made):
            own.setdefault(r, {})[begin] = value

    second = [r ^ 1 for r in first]
    parted = second + [0]
    more(second + order[0][2:3], "second_terms", last)

    for k, r in enumerate(first):
        for (begin, _), value in zip(spans, arrived_first):
            arrivals[r ^ 1].append((value[k * block_rows : (k + 1) * block_rows], begin))

    def exchange(r, spans):
        bit = (r & -r).bit_length() - 1
        for begin, end in spans:
            total = own[r][begin] if begin in own[r] and own[r][begin].shape[1] == end - begin else own[r][0][:, begin:end]
            for value, offset in arrivals[r]:
                if offset <= begin < offset + value.shape[1]:
                    total = total + wide(value[:, begin - offset : end - offset])
            last = swap_with(narrow(total), "ex", 1 << bit)
            arrivals[r ^ (1 << bit)].append((last, begin))
        return last

    left = [r for r in range(ex_count - 1, -1, -1) if r not in own and r not in first]
    began = second[: bits - 1] if len(spans) > 1 else []
    for at, r in enumerate(began):
        last = exchange(r, spans[:1])
        now, left = (left, []) if at == len(began) - 1 else (left[:-1], left[-1:])
        if now:
            more(now, f"terms_{at}", [last])
    if left:
        more(left, "last_terms", ())
    for r in order[0]:
        if r not in first:
            exchange(r, [(0, cols)])
    for bit in range(1, bits):
        for r in order[bit]:
            if r in began:
                exchange(r, spans[1:])
            else:
                exchange(r, spans if any(x.shape[1] < cols for x, _ in arrivals[r]) else [(0, cols)])

    for bit in reversed(range(bits)):
        low = (ex_index >> bit) & 1 == 0
        lower, upper = jnp.split(part, 2)
        arrived = swap_with(jnp.where(low, upper, lower), "ex", 1 << bit)
        kept = jnp.where(low, lower, upper)
        part = kept + arrived
    ends, counts = [], []
    for begin, end in spans:
        group, offsets = [own[0][begin]], []
        for value, offset in arrivals[0]:
            if offset <= begin < offset + value.shape[1]:
                group.append(value)
                offsets.append(begin - offset)
        ends += group
        counts.append((len(group), offsets))
    sketch, gradient = call(
        functools.partial(
            finish_kernel, counts, (1 / math.sqrt(sketch_count), 1 / math.sqrt(rows * ex_count))
        ),
        "finish",
        [((block_rows, cols), jnp.float32), ((1, kept.shape[0]), jnp.float32)],
        [],
        *ends,
        kept.reshape(1, -1),
        arrived.reshape(1, -1),
    )
    return margins.reshape(rows), gradient.reshape(-1), sketch


def solution(mesh):
    return jax.shard_map(
        on_device,
        mesh=mesh,
        in_specs=(P("ex", "feat"), P("ex"), P("ex"), P("ex"), P(("feat", "ex")), P()),
        out_specs=(P("ex"), P(("feat", "ex")), P("ex", "feat")),
        check_vma=False,
    )
```

```python
import functools
import math

import jax
import jax.numpy as jnp
from jax import lax
from jax.experimental import pallas as pl
from jax.experimental.pallas import tpu as pltpu
from jax.sharding import PartitionSpec as P

LANES = 128
PARAMS = pltpu.CompilerParams(vmem_limit_bytes=32 * 1024 * 1024)
NO_COST = pl.CostEstimate(flops=0, bytes_accessed=0, transcendentals=0)
ANY = pl.BlockSpec(memory_space=pl.ANY)
VMEM = pl.BlockSpec(memory_space=pltpu.VMEM)
SMEM = pl.BlockSpec(memory_space=pltpu.SMEM)


def tile_of(extent, most):
    size = most
    while extent % size:
        size //= 2
    return size


def swap_with(value, axis, distance):
    count = lax.axis_size(axis)
    return lax.ppermute(value, axis, [(i, i ^ distance) for i in range(count)])


def wide(value):
    return value.astype(jnp.float32)


def narrow(value):
    return value.astype(jnp.bfloat16)


def call(kernel, name, out_shape, scratch, *operands, scalars=(), whole=(), large=(), deps=()):
    large = [pltpu.with_memory_space_constraint(x, pltpu.VMEM) for x in large]
    used = len(scalars) + len(operands) + len(large) + len(whole)
    return pl.pallas_call(
        lambda *refs: kernel(*refs[:used], *refs[used + len(deps) :]),
        in_specs=[SMEM] * len(scalars) + [VMEM] * (len(operands) + len(large)) + [ANY] * (len(whole) + len(deps)),
        out_specs=[VMEM] * len(out_shape),
        out_shape=[jax.ShapeDtypeStruct(*entry) for entry in out_shape],
        scratch_shapes=scratch,
        compiler_params=PARAMS,
        cost_estimate=NO_COST,
        name=name,
    )(*scalars, *operands, *large, *whole, *deps)


def touch_kernel(pooled_ref, out_ref):
    out_ref[...] = pooled_ref[0:8, 0:LANES].astype(jnp.float32)


def margins_kernel(pieces, ex_ref, dir_ref, pooled_ref, out_ref, ordered_ref):
    rows, cols = pooled_ref.shape
    tile, width = tile_of(rows, 512), cols // pieces
    lanes = dir_ref.shape[1]
    for at in range(dir_ref.shape[0]):
        piece = jnp.broadcast_to(dir_ref[at : at + 1, :], (8, lanes))
        r, part = divmod(at * lanes, width)
        place = pl.ds(pl.multiple_of((ex_ref[0] ^ r) * width + part, lanes), lanes) if pieces > 1 else slice(None)
        ordered_ref[:, place] = piece
    left = ordered_ref[...].astype(jnp.bfloat16)
    for at in range(0, rows, tile):
        row = lax.dot_general(
            left, pooled_ref[at : at + tile, :], (((1,), (1,)), ((), ())), preferred_element_type=jnp.float32
        )
        for part in range(0, tile, LANES):
            group = (at + part) // LANES
            out_ref[group : group + 1, :] = row[0:1, part : part + LANES]


def sampled_rows(sampled_ref, ex_index, blocks):
    columns = []
    for r in blocks:
        row = sampled_ref[pl.ds(ex_index ^ r, 1), :]
        columns.append(jnp.broadcast_to(row, (LANES, row.shape[1])).T)
    return columns[0] if len(columns) == 1 else jnp.concatenate(columns)


def fill_signs(signs_ref, sampled, ex_index):
    high_bits = signs_ref.shape[1].bit_length() - 1
    lane = lax.broadcasted_iota(jnp.int32, sampled.shape, 1)
    folded = (sampled & lane) ^ (lax.shift_right_logical(sampled, high_bits) & ex_index)
    for shift_by in (16, 8, 4, 2, 1):
        folded = folded ^ lax.shift_right_logical(folded, shift_by)
    tiles = [(1 - 2 * (folded & 1)).astype(jnp.float32)]
    for bit in range(LANES.bit_length() - 1, high_bits):
        flip = (1 - 2 * (lax.shift_right_logical(sampled, bit) & 1)).astype(jnp.float32)
        tiles = tiles + [tile * flip for tile in tiles]
    for at, tile in enumerate(tiles):
        signs_ref[:, at * LANES : (at + 1) * LANES] = tile.astype(jnp.bfloat16)


def fill_scale(scale_col_ref, scale):
    for at in range(scale.shape[0]):
        square = jnp.broadcast_to(scale[at : at + 1, :], (LANES, LANES))
        scale_col_ref[at * LANES : (at + 1) * LANES, :] = square.T


def weigh(pooled, scale_col):
    pieces = []
    for at in range(0, pooled.shape[1], LANES):
        part = pooled[:, at : at + LANES].astype(jnp.float32)
        pieces.append((part * scale_col).astype(jnp.bfloat16))
    return pieces[0] if len(pieces) == 1 else jnp.concatenate(pieces, axis=1)


def weights_kernel(mine_ref, theirs_ref, old_ref, labels_ref, bits_ref, margins_ref, scale_ref, residual_ref):
    margins = old_ref[...] + (mine_ref[...] + theirs_ref[...])
    up, down = jax.nn.sigmoid(margins), jax.nn.sigmoid(-margins)
    margins_ref[...] = margins
    scale_ref[...] = (2 * bits_ref[...] - 1).astype(jnp.float32) * jnp.sqrt(up * down)
    residual_ref[...] = up - labels_ref[...].astype(jnp.float32)


def terms_kernel(places, blocks, with_gradient, ex_ref, scale_ref, residual_ref, sampled_ref, pooled_ref, *rest):
    *outs, signs_ref, scale_col_ref = rest
    row = jnp.concatenate([residual_ref[at : at + 1, :] for at in range(residual_ref.shape[0])], axis=1)
    residual = jnp.broadcast_to(row, (8, row.shape[1])).astype(jnp.bfloat16)
    cols = pooled_ref.shape[1]
    tile = tile_of(cols, 256)
    fill_scale(scale_col_ref, scale_ref[...])
    fill_signs(signs_ref, sampled_rows(sampled_ref, ex_ref[0], blocks), ex_ref[0])
    for at in range(0, cols, tile):
        weighted = weigh(pooled_ref[:, at : at + tile], scale_col_ref[...])
        here = [(row, col, out) for (row, col), out in zip(places, outs) if col <= at < col + out.shape[1]]
        if here:
            low = min(row for row, _, _ in here)
            high = max(row + out.shape[0] for row, _, out in here)
            terms = jnp.dot(signs_ref[low:high, :], weighted, preferred_element_type=jnp.float32)
        for row, col, out in here:
            out[:, at - col : at - col + tile] = terms[row - low : row - low + out.shape[0]].astype(out.dtype)
        if with_gradient:
            terms = jnp.dot(residual, pooled_ref[:, at : at + tile], preferred_element_type=jnp.float32)
            outs[-1][:, at : at + tile] = terms[0:1, :]


def terms_of(name, blocks, ex_scalar, scale, residual, sampled, pooled, places, outs, deps=(), with_gradient=False):
    (rows, cols), block_rows = pooled.shape, sampled.shape[1]
    if with_gradient:
        outs = [*outs, ((1, cols), jnp.float32)]
    return call(
        functools.partial(terms_kernel, places, blocks, with_gradient),
        name,
        outs,
        [
            pltpu.VMEM((len(blocks) * block_rows, rows), jnp.bfloat16),
            pltpu.VMEM((rows, LANES), jnp.float32),
        ],
        scale,
        residual,
        sampled,
        scalars=(ex_scalar,),
        large=(pooled,),
        deps=deps,
    )


def finish_kernel(counts, scales, *refs):
    *ins, sketch_ref, gradient_ref = refs
    col = 0
    ins = list(ins)
    for count, offsets in counts:
        group, ins = ins[:count], ins[count:]
        width = group[0].shape[1]
        total = group[0][...]
        for ref, offset in zip(group[1:], offsets):
            total = total + wide(ref[:, offset : offset + width])
        sketch_ref[:, col : col + width] = total * scales[0]
        col += width
    gradient_ref[...] = (ins[-2][...] + ins[-1][...]) * scales[1]


def on_device(pooled, labels, sign_bits, margins_old, direction, sample_rows):
    rows, cols = pooled.shape
    ex_count, feat_count = lax.axis_size("ex"), lax.axis_size("feat")
    bits = ex_count.bit_length() - 1
    ex_index = lax.axis_index("ex").astype(jnp.int32)
    ex_scalar = ex_index.reshape(1)
    sketch_count = sample_rows.shape[0]
    block_rows = sketch_count // ex_count
    dense = (rows // LANES, LANES)
    sampled = sample_rows.reshape(ex_count, block_rows)
    pieces = ex_count if direction.shape[0] % LANES == 0 else 1
    step_dir = direction.reshape(-1, LANES) if pieces > 1 else direction
    for bit in range(bits):
        other = swap_with(step_dir, "ex", 1 << bit)
        if bit == min(1, bits - 1):
            touched = call(touch_kernel, "touch", [((8, LANES), jnp.float32)], [], large=(pooled,), deps=[other])
        if pieces > 1:
            step_dir = jnp.concatenate([step_dir, other])
        else:
            low = (ex_index >> bit) & 1 == 0
            step_dir = jnp.concatenate([jnp.where(low, step_dir, other), jnp.where(low, other, step_dir)])

    (terms,) = call(
        functools.partial(margins_kernel, pieces),
        "margins",
        [(dense, jnp.float32)],
        [pltpu.VMEM((8, cols), jnp.float32)],
        step_dir if pieces > 1 else step_dir.reshape(1, cols),
        scalars=(ex_scalar,),
        large=(pooled,),
        deps=touched,
    )
    mine, theirs = terms, jnp.zeros_like(terms)
    distance = 1
    while distance < feat_count:
        mine, theirs = terms, swap_with(terms, "feat", distance)
        terms = mine + theirs
        distance *= 2

    margins, scale, residual = call(
        weights_kernel,
        "weights",
        [(dense, jnp.float32)] * 3,
        [],
        mine,
        theirs,
        margins_old.reshape(dense),
        labels.reshape(dense),
        sign_bits.reshape(dense),
    )
    order = [[r for r in range(ex_count - 1, 0, -1) if r & ((2 << bit) - 1) == 1 << bit] for bit in range(bits)]
    first = order[0][:2]
    cut = cols // 2 // (2 * LANES) * (2 * LANES) or cols
    spans = [(0, cut), (cut, cols)] if cut < cols else [(0, cols)]
    begin, end = spans[0]
    made = terms_of(
        "first_terms",
        first,
        ex_scalar,
        scale,
        residual,
        sampled,
        pooled,
        [(0, begin)],
        [((len(first) * block_rows, end - begin), jnp.bfloat16)],
    )
    arrived_first = [swap_with(made[0], "ex", 1)]

    own, arrivals = {}, {r: [] for r in range(ex_count)}

    def more(blocks, name, deps, together=(), with_gradient=False):
        size = len(together)
        cuts = [(k + size, r, span) for k, r in enumerate(blocks) for span in (spans if r in parted else [(0, cols)])]
        made = terms_of(
            name,
            [*together, *blocks],
            ex_scalar,
            scale,
            residual,
            sampled,
            pooled,
            [(k * block_rows, begin) for k, _, (begin, _) in cuts]
            + [(0, begin) for begin, _ in spans[1:] if together],
            [((block_rows, end - begin), jnp.bfloat16 if r & 1 else jnp.float32) for _, r, (begin, end) in cuts]
            + [((size * block_rows, end - begin), jnp.bfloat16) for begin, end in spans[1:] if together],
            deps,
            with_gradient,
        )
        for (_, r, (begin, _)), value in zip(cuts, made):
            own.setdefault(r, {})[begin] = value
        return made[len(cuts) :] or made

    second = [r ^ 1 for r in first]
    parted = second + [0]
    made = more(second, "second_terms", made, first)
    if len(spans) > 1:
        arrived_first.append(swap_with(made[0], "ex", 1))

    def gradient_round(part, bit):
        low = (ex_index >> bit) & 1 == 0
        lower, upper = jnp.split(part, 2)
        arrived = swap_with(jnp.where(low, upper, lower), "ex", 1 << bit)
        return jnp.where(low, lower, upper), arrived

    if order[0][2:3]:
        more(order[0][2:3], "third_terms", [made[0], arrived_first[0]])

    for k, r in enumerate(first):
        for (begin, _), value in zip(spans, arrived_first):
            arrivals[r ^ 1].append((value[k * block_rows : (k + 1) * block_rows], begin))

    def exchange(r, spans, behind=None):
        bit = (r & -r).bit_length() - 1
        for begin, end in spans:
            total = own[r][begin] if begin in own[r] and own[r][begin].shape[1] == end - begin else own[r][0][:, begin:end]
            for value, offset in arrivals[r]:
                if offset <= begin < offset + value.shape[1]:
                    total = total + wide(value[:, begin - offset : end - offset])
            if behind is not None:
                total = total + wide(behind) * 0
            last = swap_with(narrow(total), "ex", 1 << bit)
            arrivals[r ^ (1 << bit)].append((last, begin))
        return last

    left = [r for r in range(ex_count - 1, -1, -1) if r not in own and r not in first]
    began = second[: bits - 1] if len(spans) > 1 else []
    ahead, part = [], None
    for at, r in enumerate(began):
        last = exchange(r, spans[:1])
        ahead.append(last)
        now, left = (left, []) if at == len(began) - 1 else (left[:-1], left[-1:])
        if now:
            made = more(now, f"terms_{at}", [last], (), part is None)
            part = made[-1] if part is None else part
    if left:
        made = more(left, "last_terms", (), (), part is None)
        part = made[-1] if part is None else part
    for r in order[0]:
        if r not in first:
            exchange(r, [(0, cols)])
    for bit in range(1, bits):
        for r in order[bit]:
            if r in began:
                behind = ahead[0] if r == began[0] and ahead[0].shape[1] == cols - spans[1][0] else None
                exchange(r, spans[1:], behind)
            else:
                exchange(r, spans if any(x.shape[1] < cols for x, _ in arrivals[r]) else [(0, cols)])

    part = part.reshape(-1)
    for bit in reversed(range(bits)):
        kept, arrived = gradient_round(part, bit)
        part = kept + arrived
    ends, counts = [], []
    for begin, end in spans:
        group, offsets = [own[0][begin]], []
        for value, offset in arrivals[0]:
            if offset <= begin < offset + value.shape[1]:
                group.append(value)
                offsets.append(begin - offset)
        ends += group
        counts.append((len(group), offsets))
    sketch, gradient = call(
        functools.partial(
            finish_kernel, counts, (1 / math.sqrt(sketch_count), 1 / math.sqrt(rows * ex_count))
        ),
        "finish",
        [((block_rows, cols), jnp.float32), ((1, kept.shape[0]), jnp.float32)],
        [],
        *ends,
        kept.reshape(1, -1),
        arrived.reshape(1, -1),
    )
    return margins.reshape(rows), gradient.reshape(-1), sketch


def solution(mesh):
    return jax.shard_map(
        on_device,
        mesh=mesh,
        in_specs=(P("ex", "feat"), P("ex"), P("ex"), P("ex"), P(("feat", "ex")), P()),
        out_specs=(P("ex"), P(("feat", "ex")), P("ex", "feat")),
        check_vma=False,
    )
```
